32 devices in a mesh: height: 8 (over y, x, core), plan: 4 (over z).
Axes of the slice: x: 2, y: 2, z: 4, core: 2. Of those that a mesh axis runs over, the one named last changes fastest.
Arguments:
- divergence: float32 [32, 64, 512], P('height', 'plan'), may hold values from -8 to 8
- density: float32 [32, 64, 512], P('height', 'plan'), may hold values from 0.5 to 2
- zones: int32 [32, 64, 512], P('height', 'plan'), may hold values from 0 to 4
Outputs:
- pressure: float32 [32, 64, 512], P('height', 'plan')
The draws below stay inside these ranges and needn't reach their ends.
Inputs may be any that keep to these rules, and one draw needn't show every extreme that they name: `zones`: zone 0 open air, 1 wall, 2 stairwell, 3 open door, 4 closed door.
All inputs are finite; a program needn't handle non-finite values.
Results may differ from the reference program's by a relative error of at most 0.00002.
Values sent between devices are 32-bit elements; how exact they have to be, the bound alone decides.
A program may use at most 64 MiB of HBM per device.

```python
import math
import jax
import jax.numpy as jnp

NY = 512
PRE = 2
POST = 2
COARSE = 4
NZ = 32
NX = 64


def place_ends(entries, key, least, top_value):
    extent = entries.shape
    index_at = [jax.random.randint(jax.random.fold_in(key, axis), (), 0, extent[axis]) for axis in range(len(extent))]
    entries = entries.at[tuple(index_at)].set(least)
    longest = extent.index(max(extent))
    index_at[longest] = (index_at[longest] + 1) % extent[longest]
    return entries.at[tuple(index_at)].set(top_value)


def shard_levels(rng, dims, pieces, least, high):
    level = 1.0
    for position, blocks in pieces:
        draws = jax.random.uniform(jax.random.fold_in(jax.random.fold_in(rng, 6), position), (blocks,), jnp.float32, least / len(pieces), high / len(pieces))
        level = level * jnp.repeat(jnp.exp(draws), dims[position] // blocks).reshape((-1,) + (1,) * (len(dims) - 1 - position))
    return level


def bell_draw(stream_key, extent, deviation, reach, cuts=(), kind=jnp.bfloat16):
    values = jax.random.normal(stream_key, extent, jnp.float32) * deviation
    if len(cuts) > 0:
        values = shard_levels(stream_key, extent, cuts, -0.22, 0.18) * values
    return jnp.clip(values, min=-reach, max=reach).astype(kind)


def setup_inputs(seed: int = 0) -> dict:
    seeds = jax.random.split(jax.random.key(seed), 4)
    return {
        "divergence": bell_draw(seeds[0], (NZ, NX, NY), 1.0, 8.0, ((0, 8), (1, 4)), jnp.float32),
        "density": jnp.clip(jnp.exp(math.log(2.0) - 1.3862944 * jax.random.uniform(seeds[1], (NZ, NX, NY), jnp.float32) ** shard_levels(seeds[1], (NZ, NX, NY), ((0, 8), (1, 4)), -0.2, 0.2)), 0.5, 2.0),
        "zones": place_ends(jax.random.randint(seeds[2], (NZ, NX, NY), 0, 5), jax.random.fold_in(seeds[2], 1), 0, 4).astype(jnp.int32),
    }


PERMEABILITY = (1.0, 0.1, 0.6, 0.8, 0.25)
OMEGA = 2.0 / 3.0


def conduct(zones, density):
    perm = jnp.zeros(density.shape, jnp.float32)
    for zone_id, value in enumerate(PERMEABILITY):
        perm = perm + jnp.where(zones == zone_id, jnp.float32(value), jnp.float32(0.0))
    return perm / density


def harmonic(first, second):
    return 2.0 * first * second / (first + second)


def neighbours(padded):
    return [padded[:-2, 1:-1, 1:-1], padded[2:, 1:-1, 1:-1],
            padded[1:-1, :-2, 1:-1], padded[1:-1, 2:, 1:-1],
            padded[1:-1, 1:-1, :-2], padded[1:-1, 1:-1, 2:]]


def setup(cond, padder):
    padded = padder(cond - 1.0) + 1.0
    coeffs = [harmonic(cond, other) for other in neighbours(padded)]
    diag = coeffs[0] + coeffs[1] + coeffs[2] + coeffs[3] + coeffs[4] + coeffs[5]
    return coeffs, diag


def stencil(field, coeffs, padder):
    others = neighbours(padder(field))
    total = coeffs[0] * (field - others[0])
    for index in range(1, 6):
        total = total + coeffs[index] * (field - others[index])
    return total


def smooth(field, source, coeffs, diag, padder, count):
    for sweep in range(count):
        field = field + OMEGA * (source - stencil(field, coeffs, padder)) / diag
    return field


def block_sum(field):
    depth, across, along = field.shape
    return field.reshape(depth // 2, 2, across // 2, 2, along // 2, 2).sum(axis=(1, 3, 5))


def prolong(field):
    depth, across, along = field.shape
    wide = jnp.broadcast_to(field[:, None, :, None, :, None], (depth, 2, across, 2, along, 2))
    return wide.reshape(depth * 2, across * 2, along * 2)


def zero_pad(field):
    return jnp.pad(field, 1)


def reference(divergence, density, zones):
    cond0 = conduct(zones, density)
    coeffs0, diag0 = setup(cond0, zero_pad)
    p0 = OMEGA * divergence / diag0
    p0 = smooth(p0, divergence, coeffs0, diag0, zero_pad, PRE - 1)
    f1 = 0.5 * block_sum(divergence - stencil(p0, coeffs0, zero_pad))
    cond1 = 0.125 * block_sum(cond0)
    coeffs1, diag1 = setup(cond1, zero_pad)
    p1 = OMEGA * f1 / diag1
    p1 = smooth(p1, f1, coeffs1, diag1, zero_pad, PRE - 1)
    f2 = 0.5 * block_sum(f1 - stencil(p1, coeffs1, zero_pad))
    cond2 = 0.125 * block_sum(cond1)
    coeffs2, diag2 = setup(cond2, zero_pad)
    p2 = OMEGA * f2 / diag2
    p2 = smooth(p2, f2, coeffs2, diag2, zero_pad, COARSE - 1)
    leftover = f2 - stencil(p2, coeffs2, zero_pad)
    line = jnp.sum(leftover, axis=1, keepdims=True) / jnp.sum(diag2, axis=1, keepdims=True)
    p2 = p2 + line
    p1 = smooth(p1 + prolong(p2), f1, coeffs1, diag1, zero_pad, POST)
    p0 = smooth(p0 + prolong(p1), divergence, coeffs0, diag0, zero_pad, POST)
    return p0
```

```python
import functools

import jax
import jax.numpy as jnp
from jax import lax
from jax.experimental import pallas as pl
from jax.experimental.pallas import tpu as pltpu
from jax.sharding import PartitionSpec as P

PERMEABILITY = (1.0, 0.1, 0.6, 0.8, 0.25)
OMEGA = 2.0 / 3.0
KEEP = 1.0 / 3.0
MESH = pl.DeviceIdType.MESH
F32 = jnp.float32
LANES = 128

SIDES = (1, -1)
DIAGONALS = ((1, 1), (1, -1), (-1, 1), (-1, -1))
AROUND = tuple((a, b) for a in (-1, 0, 1) for b in (-1, 0, 1) if (a, b) != (0, 0))
WIDE = tuple((a, b) for a in (-2, -1, 0, 1, 2) for b in (-1, 0, 1) if (a, b) != (0, 0))


def harmonic(a, b):
    return 2.0 * a * b / (a + b)


def lane_of(a):
    return lax.broadcasted_iota(jnp.int32, a.shape, a.ndim - 1)


def lane_prev(a, fill):
    return jnp.where(lane_of(a) == 0, fill, pltpu.roll(a, 1, a.ndim - 1))


def lane_next(a, fill):
    return jnp.where(lane_of(a) == LANES - 1, fill, pltpu.roll(a, LANES - 1, a.ndim - 1))


def y_prev(a, fill):
    return jnp.concatenate([lane_prev(a[:, -1:], fill), a[:, :-1]], axis=1)


def y_next(a, fill):
    return jnp.concatenate([a[:, 1:], lane_next(a[:, :1], fill)], axis=1)


def x_prev(a):
    return pltpu.roll(a, 1, a.ndim - 2)


def x_next(a):
    return pltpu.roll(a, a.shape[-2] - 1, a.ndim - 2)


def setup(c, inside):
    cz = harmonic(c[:-1], c[1:])
    m = c[1:-1]
    cx = harmonic(m, x_next(m))
    cxl = x_prev(cx)
    cyl = harmonic(m, y_prev(m, 1.0))
    cyu = y_next(cyl, harmonic(m[:, -1:], jnp.ones_like(m[:, -1:])))
    diag = cz[:-1] + cz[1:] + cx + cxl + cyl + cyu
    w = jnp.where(inside, OMEGA / diag, 0.0)
    return (cz, cx, cxl, cyl, cyu, diag, w)


def trim(k):
    return tuple(part[1:-1] for part in k)


def gathered(p, k):
    cz, cx, cxl, cyl, cyu = k[:5]
    m = p[1:-1]
    return (cz[:-1] * p[:-2] + cz[1:] * p[2:] + cx * x_next(m) + cxl * x_prev(m)
            + cyl * y_prev(m, 0.0) + cyu * y_next(m, 0.0))


def sweep(p, f, k):
    return KEEP * p[1:-1] + k[6] * (f + gathered(p, k))


def residual(p, f, k):
    return f - k[5] * p[1:-1] + gathered(p, k)


def paired(a):
    z, v = a.shape[:2]
    rows = []
    for i in range(0, z, 2):
        both = a[i] + a[i + 1]
        rows.append(jnp.stack([both[q] + both[q + 1] for q in range(0, v, 2)], axis=0))
    return jnp.stack(rows, axis=0)


def split3(a):
    one = a.astype(jnp.bfloat16)
    rest = a - one.astype(F32)
    two = rest.astype(jnp.bfloat16)
    three = (rest - two.astype(F32)).astype(jnp.bfloat16)
    return jnp.concatenate([one, two, three], axis=0)


def kernel(H, PL, W, layers, window, div_ref, den_ref, zon_ref, out_ref,
           CN, DN, ZC, ZD, XS, XR, GS, GR, CA, DA, C1, F1, P1, C2O, F2O, C2G, F2G,
           PN, PZ, PXS, PXR, PGS, PGR, PA, S0, S1, Q2, Q1, P2, X2C, X2F,
           ssem, rsem, gssem, grsem):
    h = lax.axis_index("height")
    j = lax.axis_index("plan")
    base = h - W if window else 0

    def exists(dh, dj):
        ok = None
        for at, step, count in ((h, dh, H), (j, dj, PL)):
            if step > 0:
                term = at + step < count
            elif step < 0:
                term = at + step >= 0
            else:
                continue
            ok = term if ok is None else jnp.logical_and(ok, term)
        return ok

    barrier = pltpu.get_barrier_semaphore()
    if window:
        for dh in range(-W, W + 1):
            @pl.when(jnp.logical_and(h + dh >= 0, h + dh < H))
            def _():
                for dj in range(PL):
                    if (dh, dj) != (0, 0):
                        pl.semaphore_signal(barrier, inc=1, device_id=(h + dh, lax.rem(j + dj, PL)), device_id_type=MESH)
    else:
        for a in range(H):
            for b in range(PL):
                if (a, b) != (0, 0):
                    pl.semaphore_signal(barrier, inc=1, device_id=(lax.rem(h + a, H), lax.rem(j + b, PL)), device_id_type=MESH)

    zones = zon_ref[...]
    perm = jnp.zeros(zones.shape, F32)
    for zone_id, value in enumerate(PERMEABILITY):
        perm = jnp.where(zones == zone_id, F32(value), perm)
    cond = perm / den_ref[...]
    ys = lax.broadcasted_iota(jnp.int32, (512, 512), 0)
    cs = lax.broadcasted_iota(jnp.int32, (512, 512), 1)
    order = (ys == 4 * (cs % LANES) + cs // LANES).astype(F32).astype(jnp.bfloat16)
    both = jnp.concatenate([cond.reshape(64, 512), div_ref[...].reshape(64, 512)], axis=0)
    moved = jnp.dot(split3(both), order, preferred_element_type=F32)
    moved = moved[0:128] + moved[128:256] + moved[256:384]
    for v in range(4):
        part = moved[:, v * LANES:(v + 1) * LANES]
        CN[:, v] = part[0:64].reshape(4, 16, LANES)
        DN[:, v] = part[64:128].reshape(4, 16, LANES)
    c = CN[...]
    d = DN[...]
    XS[0, :, :, 0:3] = c[:, :, 13:16]
    XS[0, :, :, 3:5] = d[:, :, 14:16]
    XS[1, :, :, 0:3] = c[:, :, 0:3]
    XS[1, :, :, 3:5] = d[:, :, 0:2]
    for n, (dh, dj) in enumerate(DIAGONALS):
        near, far = (3, 2) if dh > 0 else (0, 1)
        row = 15 if dj > 0 else 0
        two = 14 if dj > 0 else 0
        GS[n, :, 0:2] = c[near, :, two:two + 2]
        GS[n, :, 2:3] = c[far, :, row:row + 1]
        GS[n, :, 3:4] = d[near, :, row:row + 1]

    index = [0]

    def copies(items):
        made = []
        for dh, dj, src, dst in items:
            n = index[0]
            index[0] += 1
            copy = pltpu.make_async_remote_copy(
                src_ref=src, dst_ref=dst, send_sem=ssem.at[n], recv_sem=rsem.at[n],
                device_id=(h + dh, j + dj), device_id_type=MESH)
            made.append((exists(dh, dj), exists(-dh, -dj), copy))
        return made

    def start(made):
        for there, _, copy in made:
            pl.when(there)(copy.start)

    def arrive(made):
        for _, back, copy in made:
            pl.when(back)(copy.wait_recv)

    def sent(made):
        for there, _, copy in made:
            pl.when(there)(copy.wait_send)

    def tiles(ref, around):
        return copies([(dh, dj, ref.at[4:6, :, 8:16], ref.at[4 - 2 * dh:6 - 2 * dh, :, 8 - 8 * dj:16 - 8 * dj])
                       for dh, dj in around])

    def gather_loop(act):
        if window:
            for dh in range(-W, W + 1):
                for b in range(PL):
                    if (dh, b) != (0, 0):
                        yes = jnp.logical_and(h + dh >= 0, h + dh < H)
                        pl.when(yes)(functools.partial(act, dh, b))
        else:
            for a in range(H):
                for b in range(PL):
                    if (a, b) != (0, 0):
                        act(a, b)

    def gather_copy(which, src, buf, a, b):
        if window:
            to, mine, n = h + a, W - a, a + W
        else:
            to, mine, n = lax.rem(h + a, H), h, a
        return pltpu.make_async_remote_copy(
            src_ref=src, dst_ref=buf.at[mine, j], send_sem=gssem.at[which, n, b],
            recv_sem=grsem.at[which, n, b], device_id=(to, lax.rem(j + b, PL)), device_id_type=MESH)

    def gather_in(which, src, buf, a, b):
        gather_copy(which, src, buf, a, b).wait_recv()

    def gather_in_loop(which, src, buf):
        if window:
            for dh in range(-W, W + 1):
                for b in range(PL):
                    if (dh, b) != (0, 0):
                        yes = jnp.logical_and(h - dh >= 0, h - dh < H)
                        pl.when(yes)(functools.partial(gather_in, which, src, buf, dh, b))
        else:
            gather_loop(functools.partial(gather_in, which, src, buf))

    count = None
    if window:
        low = jnp.minimum(h, W)
        high = jnp.minimum(H - 1 - h, W)
        count = (low + high + 1) * PL - 1
    else:
        count = H * PL - 1
    pl.semaphore_wait(barrier, count)

    first = copies(
        [(1, 0, CN.at[1:4], ZC.at[0]), (-1, 0, CN.at[0:3], ZC.at[1]),
         (1, 0, DN.at[2:4], ZD.at[0]), (-1, 0, DN.at[0:2], ZD.at[1]),
         (0, 1, XS.at[0], XR.at[0]), (0, -1, XS.at[1], XR.at[1])]
        + [(dh, dj, GS.at[n], GR.at[n]) for n, (dh, dj) in enumerate(DIAGONALS)])
    start(first)

    def pair_rows(ref, first_row, rows):
        return ref[:, :, pl.ds(first_row, rows, stride=2), :] + ref[:, :, pl.ds(first_row + 1, rows, stride=2), :]

    S0[:, :, 4:20] = paired(c)
    own1 = 0.125 * pair_rows(S0, 4, 8)
    C1[4:6, :, 8:16] = own1
    S1[:, :, 8:16] = paired(own1)
    C2O[...] = 0.125 * pair_rows(S1, 8, 4)[0, 0]
    cond1 = tiles(C1, WIDE)
    start(cond1)
    gather_loop(lambda a, b: gather_copy(0, C2O, C2G, a, b).start())

    CA[3:7, :, 4:20] = c
    DA[2:6, :, 4:20] = d
    arrive(first)
    CA[0:3, :, 4:20] = ZC[0]
    CA[7:10, :, 4:20] = ZC[1]
    DA[0:2, :, 4:20] = ZD[0]
    DA[6:8, :, 4:20] = ZD[1]
    CA[3:7, :, 1:4] = XR[0, :, :, 0:3]
    CA[3:7, :, 20:23] = XR[1, :, :, 0:3]
    DA[2:6, :, 2:4] = XR[0, :, :, 3:5]
    DA[2:6, :, 20:22] = XR[1, :, :, 3:5]
    for n, (dh, dj) in enumerate(DIAGONALS):
        near, far, dnear = (2, 1, 1) if dh > 0 else (7, 8, 6)
        two, row = (2, 3) if dj > 0 else (20, 20)
        CA[near, :, two:two + 2] = GR[n, :, 0:2]
        CA[far, :, row:row + 1] = GR[n, :, 2:3]
        DA[dnear, :, row:row + 1] = GR[n, :, 3:4]

    def inside(z_count, z_first, z_total, rows, x_first, x_total):
        z = z_first + lax.broadcasted_iota(jnp.int32, (z_count, 1, rows, LANES), 0)
        x = x_first + lax.broadcasted_iota(jnp.int32, (z_count, 1, rows, LANES), 2)
        return (z >= 0) & (z < z_total) & (x >= 0) & (x < x_total)

    in0 = inside(10, 4 * h - 3, 4 * H, 24, 16 * j - 4, 16 * PL)
    k0 = setup(jnp.where(in0, CA[...], 1.0), in0[1:-1])
    f0 = jnp.where(in0[1:-1], DA[...], 0.0)
    p = k0[6] * f0
    k0 = trim(k0)
    f0 = f0[1:-1]
    p = sweep(p, f0, k0)
    PA[1:7] = p
    k0own = trim(k0)
    f0own = f0[1:-1]
    S0[...] = paired(residual(p, f0own, k0own))
    F1[4:6, :, 8:16] = 0.5 * pair_rows(S0, 4, 8)
    second = tiles(F1, AROUND)
    start(second)

    PN[...] = p[1:5, :, 4:20]
    for z in range(4):
        PXS[0, :, z:z + 1] = p[1 + z, :, 18:19]
        PXS[1, :, z:z + 1] = p[1 + z, :, 5:6]
    for n, (dh, dj) in enumerate(DIAGONALS):
        z = 4 if dh > 0 else 1
        row = 19 if dj > 0 else 4
        PGS[n, :, 0:1] = p[z, :, row:row + 1]
    spread = copies(
        [(1, 0, PN.at[2:3], PZ.at[0]), (-1, 0, PN.at[1:2], PZ.at[1]),
         (0, 1, PXS.at[0], PXR.at[0]), (0, -1, PXS.at[1], PXR.at[1])]
        + [(dh, dj, PGS.at[n], PGR.at[n]) for n, (dh, dj) in enumerate(DIAGONALS)])
    start(spread)

    arrive(cond1)
    in1 = inside(8, 2 * h - 3, 2 * H, 24, 8 * j - 8, 8 * PL)
    k1 = setup(jnp.where(in1, C1[1:9], 1.0), in1[1:-1])
    arrive(second)
    f1 = jnp.where(in1[1:-1], F1[2:8], 0.0)
    p1 = k1[6] * f1
    k1in = trim(k1)
    f1in = f1[1:-1]
    p1 = sweep(p1, f1in, k1in)
    P1[4:6, :, 8:16] = p1[1:3, :, 8:16]
    S1[...] = paired(residual(p1, f1in[1:-1], trim(k1in)))
    F2O[...] = 0.5 * pair_rows(S1, 8, 4)[0, 0]
    gather_loop(lambda a, b: gather_copy(1, F2O, F2G, a, b).start())
    third = tiles(P1, WIDE)
    start(third)

    def own_slot(ref):
        return ref.at[W if window else h, j]

    own_slot(C2G)[...] = C2O[...]
    own_slot(F2G)[...] = F2O[...]
    gather_in_loop(0, C2O, C2G)
    for b in range(PL):
        X2C[:, 4 * b:4 * b + 4, :] = C2G[:, b]
    zz = base + lax.broadcasted_iota(jnp.int32, (layers, 4 * PL, LANES), 0)
    in2 = (zz >= 0) & (zz < H)
    row = lax.broadcasted_iota(jnp.int32, (layers, 4 * PL, LANES), 1)

    def z_prev2(a, fill):
        return jnp.concatenate([jnp.full_like(a[:1], fill), a[:-1]], axis=0)

    def z_next2(a, fill):
        return jnp.concatenate([a[1:], jnp.full_like(a[:1], fill)], axis=0)

    def x_prev2(a, fill):
        return jnp.where(row == 0, fill, x_prev(a))

    def x_next2(a, fill):
        return jnp.where(row == 4 * PL - 1, fill, x_next(a))

    c2 = jnp.where(in2, X2C[...], 1.0)
    edge = harmonic(c2, jnp.ones_like(c2))
    zl = harmonic(c2, z_prev2(c2, 1.0))
    zu = jnp.concatenate([zl[1:], edge[-1:]], axis=0)
    xl = harmonic(c2, x_prev2(c2, 1.0))
    xu = jnp.where(row == 4 * PL - 1, edge, x_next(xl))
    yl = harmonic(c2, lane_prev(c2, 1.0))
    yu = lane_next(yl, edge)
    diag2 = zl + zu + xl + xu + yl + yu
    w2 = jnp.where(in2, OMEGA / diag2, 0.0)
    share = jnp.sum(diag2, axis=1, keepdims=True)

    def gathered2(q):
        return (zl * z_prev2(q, 0.0) + zu * z_next2(q, 0.0) + xl * x_prev2(q, 0.0) + xu * x_next2(q, 0.0)
                + yl * lane_prev(q, 0.0) + yu * lane_next(q, 0.0))

    gather_in_loop(1, F2O, F2G)
    for b in range(PL):
        X2F[:, 4 * b:4 * b + 4, :] = F2G[:, b]
    f2 = jnp.where(in2, X2F[...], 0.0)
    p2 = w2 * f2
    for _ in range(3):
        p2 = KEEP * p2 + w2 * (f2 + gathered2(p2))
    r2 = f2 - diag2 * p2 + gathered2(p2)
    line = jnp.sum(r2, axis=1, keepdims=True) / share
    p2 = jnp.where(in2, p2 + line, 0.0)
    blank = jnp.zeros((2, 4 * PL, LANES), F32)
    P2[0:2] = blank
    P2[2:2 + layers] = p2
    P2[2 + layers:4 + layers] = blank
    near2 = P2[pl.ds(W if window else h, 5)]
    side = jnp.zeros((5, 4, LANES), F32)
    wide2 = jnp.concatenate([side, near2, side], axis=1)
    mine2 = wide2[:, 0:12]
    for b in range(1, PL):
        mine2 = jnp.where(j == b, wide2[:, 4 * b:4 * b + 12], mine2)
    Q2[:, pl.ds(0, 12, stride=2), :] = mine2
    Q2[:, pl.ds(1, 12, stride=2), :] = mine2
    up2 = Q2[...]
    up2 = jnp.stack([up2[q] for q in (0, 1, 1, 2, 2, 3, 3, 4)], axis=0)[:, None]

    arrive(third)
    p1 = jnp.where(in1, P1[1:9] + up2, 0.0)
    p1 = sweep(p1, f1, k1)
    p1 = sweep(p1, f1in, k1in)
    Q1[:, :, pl.ds(0, 12, stride=2), :] = p1[:, :, 6:18]
    Q1[:, :, pl.ds(1, 12, stride=2), :] = p1[:, :, 6:18]
    up1 = Q1[...]

    arrive(spread)
    PA[0, :, 4:20] = PZ[0, 0]
    PA[7, :, 4:20] = PZ[1, 0]
    for z in range(4):
        PA[2 + z, :, 2:3] = PXR[0, :, z:z + 1]
        PA[2 + z, :, 21:22] = PXR[1, :, z:z + 1]
    for n, (dh, dj) in enumerate(DIAGONALS):
        z = 1 if dh > 0 else 6
        at = 3 if dj > 0 else 20
        PA[z, :, at:at + 1] = PGR[n, :, 0:1]
    fine = jnp.stack([jnp.stack([up1[z // 2, v // 2] for v in range(4)], axis=0) for z in range(8)], axis=0)
    p = jnp.where(in0[1:-1], PA[...] + fine, 0.0)
    p = sweep(p, f0, k0)
    p = sweep(p, f0own, k0own)
    p = p[:, :, 4:20]
    flat = jnp.concatenate([p[:, v].reshape(64, LANES) for v in range(4)], axis=1)
    back = lax.dot_general(split3(flat), order, (((1,), (1,)), ((), ())), preferred_element_type=F32)
    out_ref[...] = (back[0:64] + back[64:128] + back[128:192]).reshape(4, 16, 512)

    for made in (first, cond1, second, spread, third):
        sent(made)
    gather_loop(lambda a, b: gather_copy(0, C2O, C2G, a, b).wait_send())
    gather_loop(lambda a, b: gather_copy(1, F2O, F2G, a, b).wait_send())


def solution(mesh):
    H = mesh.shape["height"]
    PL = mesh.shape["plan"]
    window = H > 15
    W = 7
    layers = 2 * W + 1 if window else H
    copies = 10 + len(WIDE) + len(AROUND) + 8 + len(WIDE)

    def v(*shape):
        return pltpu.VMEM(shape + (LANES,), F32)

    scratch = [
        v(4, 4, 16), v(4, 4, 16),
        v(2, 3, 4, 16), v(2, 2, 4, 16),
        v(2, 4, 4, 8), v(2, 4, 4, 8),
        v(4, 4, 8), v(4, 4, 8),
        v(10, 4, 24), v(8, 4, 24),
        v(10, 2, 24), v(10, 2, 24), v(10, 2, 24),
        v(4), v(4), v(layers, PL, 4), v(layers, PL, 4),
        v(4, 4, 16), v(2, 1, 4, 16),
        v(2, 4, 8), v(2, 4, 8),
        v(4, 4, 8), v(4, 4, 8),
        v(8, 4, 24),
        v(2, 2, 24), v(1, 1, 24),
        v(5, 24), v(4, 2, 24),
        v(layers + 4, 4 * PL), v(layers, 4 * PL), v(layers, 4 * PL),
        pltpu.SemaphoreType.DMA((copies,)), pltpu.SemaphoreType.DMA((copies,)),
        pltpu.SemaphoreType.DMA((2, layers, PL)), pltpu.SemaphoreType.DMA((2, layers, PL)),
    ]

    def on_device(divergence, density, zones):
        return pl.pallas_call(
            functools.partial(kernel, H, PL, W, layers, window),
            out_shape=jax.ShapeDtypeStruct(divergence.shape, F32),
            in_specs=[pl.BlockSpec(memory_space=pltpu.VMEM)] * 3,
            out_specs=pl.BlockSpec(memory_space=pltpu.VMEM),
            scratch_shapes=scratch,
            compiler_params=pltpu.CompilerParams(
                collective_id=0, has_side_effects=True, vmem_limit_bytes=48 * 1024 * 1024),
            cost_estimate=pl.CostEstimate(flops=20_000_000, bytes_accessed=1_000_000, transcendentals=0),
            name="v_cycle",
        )(divergence, density, zones)

    spec = P("height", "plan", None)
    return jax.shard_map(on_device, mesh=mesh, in_specs=(spec, spec, spec), out_specs=spec, check_vma=False)
```

```python
import functools

import jax
import jax.numpy as jnp
from jax import lax
from jax.experimental import pallas as pl
from jax.experimental.pallas import tpu as pltpu
from jax.sharding import PartitionSpec as P

PERMEABILITY = (1.0, 0.1, 0.6, 0.8, 0.25)
OMEGA = 2.0 / 3.0
KEEP = 1.0 / 3.0
MESH = pl.DeviceIdType.MESH
F32 = jnp.float32
LANES = 128

SIDES = (1, -1)
DIAGONALS = ((1, 1), (1, -1), (-1, 1), (-1, -1))
AROUND = tuple((a, b) for a in (-1, 0, 1) for b in (-1, 0, 1) if (a, b) != (0, 0))
WIDE = tuple((a, b) for a in (-2, -1, 0, 1, 2) for b in (-1, 0, 1) if (a, b) != (0, 0))


def inverse(a):
    r = pl.reciprocal(a, approx=True)
    return r * (2.0 - a * r)


def harmonic(a, b):
    return (2.0 * a * b) * inverse(a + b)


def wrap(a, count):
    return jnp.where(a >= count, a - count, a)


def lane_of(a):
    return lax.broadcasted_iota(jnp.int32, a.shape, a.ndim - 1)


def lane_prev(a, fill):
    return jnp.where(lane_of(a) == 0, fill, pltpu.roll(a, 1, a.ndim - 1))


def lane_next(a, fill):
    return jnp.where(lane_of(a) == LANES - 1, fill, pltpu.roll(a, LANES - 1, a.ndim - 1))


def y_prev(a, fill):
    return jnp.concatenate([lane_prev(a[:, -1:], fill), a[:, :-1]], axis=1)


def y_next(a, fill):
    return jnp.concatenate([a[:, 1:], lane_next(a[:, :1], fill)], axis=1)


def x_prev(a):
    return pltpu.roll(a, 1, a.ndim - 2)


def x_next(a):
    return pltpu.roll(a, a.shape[-2] - 1, a.ndim - 2)


def setup(c, inside):
    cz = harmonic(c[:-1], c[1:])
    m = c[1:-1]
    cx = harmonic(m, x_next(m))
    cxl = x_prev(cx)
    cyl = harmonic(m, y_prev(m, 1.0))
    cyu = y_next(cyl, harmonic(m[:, -1:], jnp.ones_like(m[:, -1:])))
    diag = cz[:-1] + cz[1:] + cx + cxl + cyl + cyu
    w = jnp.where(inside, OMEGA * inverse(diag), 0.0)
    return (cz, cx, cxl, cyl, cyu, diag, w)


def trim(k):
    return tuple(part[1:-1] for part in k)


def gathered(p, k):
    cz, cx, cxl, cyl, cyu = k[:5]
    m = p[1:-1]
    return (cz[:-1] * p[:-2] + cz[1:] * p[2:] + cx * x_next(m) + cxl * x_prev(m)
            + cyl * y_prev(m, 0.0) + cyu * y_next(m, 0.0))


def sweep(p, f, k):
    return KEEP * p[1:-1] + k[6] * (f + gathered(p, k))


def residual(p, f, k):
    return f - k[5] * p[1:-1] + gathered(p, k)


def paired(a):
    z, v = a.shape[:2]
    rows = []
    for i in range(0, z, 2):
        both = a[i] + a[i + 1]
        rows.append(jnp.stack([both[q] + both[q + 1] for q in range(0, v, 2)], axis=0))
    return jnp.stack(rows, axis=0)


def split3(a):
    one = a.astype(jnp.bfloat16)
    rest = a - one.astype(F32)
    two = rest.astype(jnp.bfloat16)
    three = (rest - two.astype(F32)).astype(jnp.bfloat16)
    return jnp.concatenate([one, two, three], axis=0)


def kernel(H, PL, W, layers, window, div_ref, den_ref, zon_ref, out_ref,
           CN, DN, ZC, ZD, XS, XR, GS, GR, CA, DA, C1, F1, P1, C2O, F2O, C2G, F2G,
           PN, PZ, PXS, PXR, PGS, PGR, PA, S0, S1, Q2, Q1, P2, X2C, X2F,
           DIN, ZIN, VIN, ssem, rsem, gssem, grsem, isem):
    loads = [pltpu.make_async_copy(src, dst, isem.at[n])
             for n, (src, dst) in enumerate(((zon_ref, ZIN), (den_ref, DIN), (div_ref, VIN)))]
    for load in loads:
        load.start()
    h = lax.axis_index("height")
    j = lax.axis_index("plan")
    base = h - W if window else 0

    def exists(dh, dj):
        ok = None
        for at, step, count in ((h, dh, H), (j, dj, PL)):
            if step > 0:
                term = at + step < count
            elif step < 0:
                term = at + step >= 0
            else:
                continue
            ok = term if ok is None else jnp.logical_and(ok, term)
        return ok

    barrier = pltpu.get_barrier_semaphore()
    if window:
        for dh in range(-W, W + 1):
            @pl.when(jnp.logical_and(h + dh >= 0, h + dh < H))
            def _():
                for dj in range(PL):
                    if (dh, dj) != (0, 0):
                        pl.semaphore_signal(barrier, inc=1, device_id=(h + dh, wrap(j + dj, PL)), device_id_type=MESH)
    else:
        for a in range(H):
            for b in range(PL):
                if (a, b) != (0, 0):
                    pl.semaphore_signal(barrier, inc=1, device_id=(wrap(h + a, H), wrap(j + b, PL)), device_id_type=MESH)

    ys = lax.broadcasted_iota(jnp.int32, (512, 512), 0)
    cs = lax.broadcasted_iota(jnp.int32, (512, 512), 1)
    order = (ys == 4 * (cs % LANES) + cs // LANES).astype(F32).astype(jnp.bfloat16)
    for load in loads:
        load.wait()
    zones = ZIN[...]
    perm = jnp.zeros(zones.shape, F32)
    for zone_id, value in enumerate(PERMEABILITY):
        perm = jnp.where(zones == zone_id, F32(value), perm)
    cond = perm * inverse(DIN[...])
    both = jnp.concatenate([cond.reshape(64, 512), VIN[...].reshape(64, 512)], axis=0)
    moved = jnp.dot(split3(both), order, preferred_element_type=F32)
    moved = moved[0:128] + moved[128:256] + moved[256:384]
    for v in range(4):
        part = moved[:, v * LANES:(v + 1) * LANES]
        CN[:, v] = part[0:64].reshape(4, 16, LANES)
        DN[:, v] = part[64:128].reshape(4, 16, LANES)
    c = CN[...]
    d = DN[...]
    XS[0, :, :, 0:3] = c[:, :, 13:16]
    XS[0, :, :, 3:5] = d[:, :, 14:16]
    XS[1, :, :, 0:3] = c[:, :, 0:3]
    XS[1, :, :, 3:5] = d[:, :, 0:2]
    for n, (dh, dj) in enumerate(DIAGONALS):
        near, far = (3, 2) if dh > 0 else (0, 1)
        row = 15 if dj > 0 else 0
        two = 14 if dj > 0 else 0
        GS[n, :, 0:2] = c[near, :, two:two + 2]
        GS[n, :, 2:3] = c[far, :, row:row + 1]
        GS[n, :, 3:4] = d[near, :, row:row + 1]

    index = [0]

    def copies(items):
        made = []
        for dh, dj, src, dst in items:
            n = index[0]
            index[0] += 1
            copy = pltpu.make_async_remote_copy(
                src_ref=src, dst_ref=dst, send_sem=ssem.at[n], recv_sem=rsem.at[n],
                device_id=(h + dh, j + dj), device_id_type=MESH)
            made.append((exists(dh, dj), exists(-dh, -dj), copy))
        return made

    def start(made):
        for there, _, copy in made:
            pl.when(there)(copy.start)

    def arrive(made):
        for _, back, copy in made:
            pl.when(back)(copy.wait_recv)

    def sent(made):
        for there, _, copy in made:
            pl.when(there)(copy.wait_send)

    def tiles(ref, around, rows):
        items = []
        for dh, dj in around:
            z0, z1 = {2: (5, 6), -2: (4, 5)}.get(dh, (4, 6))
            x0, x1 = {1: (16 - rows, 16), -1: (8, 8 + rows)}.get(dj, (8, 16))
            items.append((dh, dj, ref.at[z0:z1, :, x0:x1],
                          ref.at[z0 - 2 * dh:z1 - 2 * dh, :, x0 - 8 * dj:x1 - 8 * dj]))
        return copies(items)

    def gather_loop(act):
        if window:
            for dh in range(-W, W + 1):
                for b in range(PL):
                    if (dh, b) != (0, 0):
                        yes = jnp.logical_and(h + dh >= 0, h + dh < H)
                        pl.when(yes)(functools.partial(act, dh, b))
        else:
            for a in range(H):
                for b in range(PL):
                    if (a, b) != (0, 0):
                        act(a, b)

    def gather_copy(which, src, buf, a, b):
        if window:
            to, mine, n = h + a, W - a, a + W
        else:
            to, mine, n = wrap(h + a, H), h, a
        return pltpu.make_async_remote_copy(
            src_ref=src, dst_ref=buf.at[mine, j], send_sem=gssem.at[which, n, b],
            recv_sem=grsem.at[which, n, b], device_id=(to, wrap(j + b, PL)), device_id_type=MESH)

    def gather_in(which, src, buf, a, b):
        gather_copy(which, src, buf, a, b).wait_recv()

    def gather_in_loop(which, src, buf):
        if window:
            for dh in range(-W, W + 1):
                for b in range(PL):
                    if (dh, b) != (0, 0):
                        yes = jnp.logical_and(h - dh >= 0, h - dh < H)
                        pl.when(yes)(functools.partial(gather_in, which, src, buf, dh, b))
        else:
            gather_loop(functools.partial(gather_in, which, src, buf))

    count = None
    if window:
        low = jnp.minimum(h, W)
        high = jnp.minimum(H - 1 - h, W)
        count = (low + high + 1) * PL - 1
    else:
        count = H * PL - 1
    pl.semaphore_wait(barrier, count)

    first = copies(
        [(1, 0, CN.at[1:4], ZC.at[0]), (-1, 0, CN.at[0:3], ZC.at[1]),
         (1, 0, DN.at[2:4], ZD.at[0]), (-1, 0, DN.at[0:2], ZD.at[1]),
         (0, 1, XS.at[0, :, :, 0:5], XR.at[0, :, :, 0:5]), (0, -1, XS.at[1, :, :, 0:5], XR.at[1, :, :, 0:5])]
        + [(dh, dj, GS.at[n, :, 0:4], GR.at[n, :, 0:4]) for n, (dh, dj) in enumerate(DIAGONALS)])
    start(first)

    def pair_rows(ref, first_row, rows):
        return ref[:, :, pl.ds(first_row, rows, stride=2), :] + ref[:, :, pl.ds(first_row + 1, rows, stride=2), :]

    S0[:, :, 4:20] = paired(c)
    own1 = 0.125 * pair_rows(S0, 4, 8)
    C1[4:6, :, 8:16] = own1
    S1[:, :, 8:16] = paired(own1)
    C2O[...] = 0.125 * pair_rows(S1, 8, 4)[0, 0]
    cond1 = tiles(C1, WIDE, 3)
    start(cond1)
    gather_loop(lambda a, b: gather_copy(0, C2O, C2G, a, b).start())

    CA[3:7, :, 4:20] = c
    DA[2:6, :, 4:20] = d
    arrive(first)
    CA[0:3, :, 4:20] = ZC[0]
    CA[7:10, :, 4:20] = ZC[1]
    DA[0:2, :, 4:20] = ZD[0]
    DA[6:8, :, 4:20] = ZD[1]
    CA[3:7, :, 1:4] = XR[0, :, :, 0:3]
    CA[3:7, :, 20:23] = XR[1, :, :, 0:3]
    DA[2:6, :, 2:4] = XR[0, :, :, 3:5]
    DA[2:6, :, 20:22] = XR[1, :, :, 3:5]
    for n, (dh, dj) in enumerate(DIAGONALS):
        near, far, dnear = (2, 1, 1) if dh > 0 else (7, 8, 6)
        two, row = (2, 3) if dj > 0 else (20, 20)
        CA[near, :, two:two + 2] = GR[n, :, 0:2]
        CA[far, :, row:row + 1] = GR[n, :, 2:3]
        DA[dnear, :, row:row + 1] = GR[n, :, 3:4]

    def inside(z_count, z_first, z_total, rows, x_first, x_total):
        z = z_first + lax.broadcasted_iota(jnp.int32, (z_count, 1, rows, LANES), 0)
        x = x_first + lax.broadcasted_iota(jnp.int32, (z_count, 1, rows, LANES), 2)
        return (z >= 0) & (z < z_total) & (x >= 0) & (x < x_total)

    in0 = inside(10, 4 * h - 3, 4 * H, 24, 16 * j - 4, 16 * PL)
    k0 = setup(jnp.where(in0, CA[...], 1.0), in0[1:-1])
    f0 = jnp.where(in0[1:-1], DA[...], 0.0)
    p = k0[6] * f0
    k0 = trim(k0)
    f0 = f0[1:-1]
    p = sweep(p, f0, k0)
    PA[1:7] = p
    k0own = trim(k0)
    f0own = f0[1:-1]
    S0[...] = paired(residual(p, f0own, k0own))
    F1[4:6, :, 8:16] = 0.5 * pair_rows(S0, 4, 8)
    second = tiles(F1, AROUND, 2)
    start(second)

    PN[...] = p[1:5, :, 4:20]
    for z in range(4):
        PXS[0, :, z:z + 1] = p[1 + z, :, 18:19]
        PXS[1, :, z:z + 1] = p[1 + z, :, 5:6]
    for n, (dh, dj) in enumerate(DIAGONALS):
        z = 4 if dh > 0 else 1
        row = 19 if dj > 0 else 4
        PGS[n, :, 0:1] = p[z, :, row:row + 1]
    spread = copies(
        [(1, 0, PN.at[2:3], PZ.at[0]), (-1, 0, PN.at[1:2], PZ.at[1]),
         (0, 1, PXS.at[0, :, 0:4], PXR.at[0, :, 0:4]), (0, -1, PXS.at[1, :, 0:4], PXR.at[1, :, 0:4])]
        + [(dh, dj, PGS.at[n, :, 0:1], PGR.at[n, :, 0:1]) for n, (dh, dj) in enumerate(DIAGONALS)])
    start(spread)

    arrive(cond1)
    in1 = inside(8, 2 * h - 3, 2 * H, 24, 8 * j - 8, 8 * PL)
    k1 = setup(jnp.where(in1, C1[1:9], 1.0), in1[1:-1])
    arrive(second)
    f1 = jnp.where(in1[1:-1], F1[2:8], 0.0)
    p1 = k1[6] * f1
    k1in = trim(k1)
    f1in = f1[1:-1]
    p1 = sweep(p1, f1in, k1in)
    P1[4:6, :, 8:16] = p1[1:3, :, 8:16]
    S1[...] = paired(residual(p1, f1in[1:-1], trim(k1in)))
    F2O[...] = 0.5 * pair_rows(S1, 8, 4)[0, 0]
    gather_loop(lambda a, b: gather_copy(1, F2O, F2G, a, b).start())
    third = tiles(P1, WIDE, 3)
    start(third)

    def own_slot(ref):
        return ref.at[W if window else h, j]

    own_slot(C2G)[...] = C2O[...]
    own_slot(F2G)[...] = F2O[...]
    gather_in_loop(0, C2O, C2G)
    for b in range(PL):
        X2C[:, 4 * b:4 * b + 4, :] = C2G[:, b]
    zz = base + lax.broadcasted_iota(jnp.int32, (layers, 4 * PL, LANES), 0)
    in2 = (zz >= 0) & (zz < H)
    row = lax.broadcasted_iota(jnp.int32, (layers, 4 * PL, LANES), 1)

    def z_prev2(a, fill):
        return jnp.concatenate([jnp.full_like(a[:1], fill), a[:-1]], axis=0)

    def z_next2(a, fill):
        return jnp.concatenate([a[1:], jnp.full_like(a[:1], fill)], axis=0)

    def x_prev2(a, fill):
        return jnp.where(row == 0, fill, x_prev(a))

    def x_next2(a, fill):
        return jnp.where(row == 4 * PL - 1, fill, x_next(a))

    c2 = jnp.where(in2, X2C[...], 1.0)
    edge = harmonic(c2, jnp.ones_like(c2))
    zl = harmonic(c2, z_prev2(c2, 1.0))
    zu = jnp.concatenate([zl[1:], edge[-1:]], axis=0)
    xl = harmonic(c2, x_prev2(c2, 1.0))
    xu = jnp.where(row == 4 * PL - 1, edge, x_next(xl))
    yl = harmonic(c2, lane_prev(c2, 1.0))
    yu = lane_next(yl, edge)
    diag2 = zl + zu + xl + xu + yl + yu
    w2 = jnp.where(in2, OMEGA * inverse(diag2), 0.0)
    share = jnp.sum(diag2, axis=1, keepdims=True)

    def gathered2(q):
        return (zl * z_prev2(q, 0.0) + zu * z_next2(q, 0.0) + xl * x_prev2(q, 0.0) + xu * x_next2(q, 0.0)
                + yl * lane_prev(q, 0.0) + yu * lane_next(q, 0.0))

    gather_in_loop(1, F2O, F2G)
    for b in range(PL):
        X2F[:, 4 * b:4 * b + 4, :] = F2G[:, b]
    f2 = jnp.where(in2, X2F[...], 0.0)
    p2 = w2 * f2
    for _ in range(3):
        p2 = KEEP * p2 + w2 * (f2 + gathered2(p2))
    r2 = f2 - diag2 * p2 + gathered2(p2)
    line = jnp.sum(r2, axis=1, keepdims=True) / share
    p2 = jnp.where(in2, p2 + line, 0.0)
    blank = jnp.zeros((2, 4 * PL, LANES), F32)
    P2[0:2] = blank
    P2[2:2 + layers] = p2
    P2[2 + layers:4 + layers] = blank
    near2 = P2[pl.ds(W if window else h, 5)]
    side = jnp.zeros((5, 4, LANES), F32)
    wide2 = jnp.concatenate([side, near2, side], axis=1)
    mine2 = wide2[:, 0:12]
    for b in range(1, PL):
        mine2 = jnp.where(j == b, wide2[:, 4 * b:4 * b + 12], mine2)
    Q2[:, pl.ds(0, 12, stride=2), :] = mine2
    Q2[:, pl.ds(1, 12, stride=2), :] = mine2
    up2 = Q2[...]
    up2 = jnp.stack([up2[q] for q in (0, 1, 1, 2, 2, 3, 3, 4)], axis=0)[:, None]

    arrive(third)
    p1 = jnp.where(in1, P1[1:9] + up2, 0.0)
    p1 = sweep(p1, f1, k1)
    p1 = sweep(p1, f1in, k1in)
    Q1[:, :, pl.ds(0, 12, stride=2), :] = p1[:, :, 6:18]
    Q1[:, :, pl.ds(1, 12, stride=2), :] = p1[:, :, 6:18]
    up1 = Q1[...]

    arrive(spread)
    PA[0, :, 4:20] = PZ[0, 0]
    PA[7, :, 4:20] = PZ[1, 0]
    for z in range(4):
        PA[2 + z, :, 2:3] = PXR[0, :, z:z + 1]
        PA[2 + z, :, 21:22] = PXR[1, :, z:z + 1]
    for n, (dh, dj) in enumerate(DIAGONALS):
        z = 1 if dh > 0 else 6
        at = 3 if dj > 0 else 20
        PA[z, :, at:at + 1] = PGR[n, :, 0:1]
    fine = jnp.stack([jnp.stack([up1[z // 2, v // 2] for v in range(4)], axis=0) for z in range(8)], axis=0)
    p = jnp.where(in0[1:-1], PA[...] + fine, 0.0)
    p = sweep(p, f0, k0)
    p = sweep(p, f0own, k0own)
    p = p[:, :, 4:20]
    flat = jnp.concatenate([p[:, v].reshape(64, LANES) for v in range(4)], axis=1)
    back = lax.dot_general(split3(flat), order, (((1,), (1,)), ((), ())), preferred_element_type=F32)
    out_ref[...] = (back[0:64] + back[64:128] + back[128:192]).reshape(4, 16, 512)

    for made in (first, cond1, second, spread, third):
        sent(made)
    gather_loop(lambda a, b: gather_copy(0, C2O, C2G, a, b).wait_send())
    gather_loop(lambda a, b: gather_copy(1, F2O, F2G, a, b).wait_send())


def solution(mesh):
    H = mesh.shape["height"]
    PL = mesh.shape["plan"]
    window = H > 15
    W = 7
    layers = 2 * W + 1 if window else H
    copies = 10 + len(WIDE) + len(AROUND) + 8 + len(WIDE)

    def v(*shape):
        return pltpu.VMEM(shape + (LANES,), F32)

    scratch = [
        v(4, 4, 16), v(4, 4, 16),
        v(2, 3, 4, 16), v(2, 2, 4, 16),
        v(2, 4, 4, 8), v(2, 4, 4, 8),
        v(4, 4, 8), v(4, 4, 8),
        v(10, 4, 24), v(8, 4, 24),
        v(10, 2, 24), v(10, 2, 24), v(10, 2, 24),
        v(4), v(4), v(layers, PL, 4), v(layers, PL, 4),
        v(4, 4, 16), v(2, 1, 4, 16),
        v(2, 4, 8), v(2, 4, 8),
        v(4, 4, 8), v(4, 4, 8),
        v(8, 4, 24),
        v(2, 2, 24), v(1, 1, 24),
        v(5, 24), v(4, 2, 24),
        v(layers + 4, 4 * PL), v(layers, 4 * PL), v(layers, 4 * PL),
        pltpu.VMEM((4, 16, 512), F32), pltpu.VMEM((4, 16, 512), jnp.int32), pltpu.VMEM((4, 16, 512), F32),
        pltpu.SemaphoreType.DMA((copies,)), pltpu.SemaphoreType.DMA((copies,)),
        pltpu.SemaphoreType.DMA((2, layers, PL)), pltpu.SemaphoreType.DMA((2, layers, PL)),
        pltpu.SemaphoreType.DMA((3,)),
    ]

    def on_device(divergence, density, zones):
        return pl.pallas_call(
            functools.partial(kernel, H, PL, W, layers, window),
            out_shape=jax.ShapeDtypeStruct(divergence.shape, F32),
            in_specs=[pl.BlockSpec(memory_space=pltpu.HBM)] * 3,
            out_specs=pl.BlockSpec(memory_space=pltpu.VMEM),
            scratch_shapes=scratch,
            compiler_params=pltpu.CompilerParams(
                collective_id=0, has_side_effects=True, vmem_limit_bytes=48 * 1024 * 1024),
            cost_estimate=pl.CostEstimate(flops=20_000_000, bytes_accessed=1_000_000, transcendentals=0),
            name="v_cycle",
        )(divergence, density, zones)

    spec = P("height", "plan", None)
    return jax.shard_map(on_device, mesh=mesh, in_specs=(spec, spec, spec), out_specs=spec, check_vma=False)
```

```python
import functools

import jax
import jax.numpy as jnp
from jax import lax
from jax.experimental import pallas as pl
from jax.experimental.pallas import tpu as pltpu
from jax.sharding import PartitionSpec as P

PERMEABILITY = (1.0, 0.1, 0.6, 0.8, 0.25)
OMEGA = 2.0 / 3.0
KEEP = 1.0 / 3.0
MESH = pl.DeviceIdType.MESH
F32 = jnp.float32
LANES = 128

SIDES = (1, -1)
DIAGONALS = ((1, 1), (1, -1), (-1, 1), (-1, -1))
AROUND = tuple((a, b) for a in (-1, 0, 1) for b in (-1, 0, 1) if (a, b) != (0, 0))
WIDE = tuple((a, b) for a in (-2, -1, 0, 1, 2) for b in (-1, 0, 1) if (a, b) != (0, 0))


def inverse(a):
    r = pl.reciprocal(a, approx=True)
    return r * (2.0 - a * r)


def harmonic(a, b):
    return (2.0 * a * b) * inverse(a + b)


def wrap(a, count):
    return jnp.where(a >= count, a - count, a)


def lane_of(a):
    return lax.broadcasted_iota(jnp.int32, a.shape, a.ndim - 1)


def lane_prev(a, fill):
    return jnp.where(lane_of(a) == 0, fill, pltpu.roll(a, 1, a.ndim - 1))


def lane_next(a, fill):
    return jnp.where(lane_of(a) == LANES - 1, fill, pltpu.roll(a, LANES - 1, a.ndim - 1))


def y_prev(a, fill):
    return jnp.concatenate([lane_prev(a[:, -1:], fill), a[:, :-1]], axis=1)


def y_next(a, fill):
    return jnp.concatenate([a[:, 1:], lane_next(a[:, :1], fill)], axis=1)


def x_prev(a):
    return pltpu.roll(a, 1, a.ndim - 2)


def x_next(a):
    return pltpu.roll(a, a.shape[-2] - 1, a.ndim - 2)


def setup(c, inside):
    cz = harmonic(c[:-1], c[1:])
    m = c[1:-1]
    cx = harmonic(m, x_next(m))
    cxl = x_prev(cx)
    cyl = harmonic(m, y_prev(m, 1.0))
    cyu = y_next(cyl, harmonic(m[:, -1:], jnp.ones_like(m[:, -1:])))
    diag = cz[:-1] + cz[1:] + cx + cxl + cyl + cyu
    w = jnp.where(inside, OMEGA * inverse(diag), 0.0)
    return (cz, cx, cxl, cyl, cyu, diag, w)


def trim(k):
    return tuple(part[1:-1] for part in k)


def gathered(p, k):
    cz, cx, cxl, cyl, cyu = k[:5]
    m = p[1:-1]
    return (cz[:-1] * p[:-2] + cz[1:] * p[2:] + cx * x_next(m) + cxl * x_prev(m)
            + cyl * y_prev(m, 0.0) + cyu * y_next(m, 0.0))


def sweep(p, f, k):
    return KEEP * p[1:-1] + k[6] * (f + gathered(p, k))


def residual(p, f, k):
    return f - k[5] * p[1:-1] + gathered(p, k)


def paired(a):
    z, v = a.shape[:2]
    rows = []
    for i in range(0, z, 2):
        both = a[i] + a[i + 1]
        rows.append(jnp.stack([both[q] + both[q + 1] for q in range(0, v, 2)], axis=0))
    return jnp.stack(rows, axis=0)


def split3(a):
    one = a.astype(jnp.bfloat16)
    rest = a - one.astype(F32)
    two = rest.astype(jnp.bfloat16)
    three = (rest - two.astype(F32)).astype(jnp.bfloat16)
    return jnp.concatenate([one, two, three], axis=0)


def kernel(H, PL, W, layers, window, div_ref, den_ref, zon_ref, out_ref,
           CN, DN, ZC, ZD, XS, XR, GS, GR, CA, DA, C1, F1, P1, C2O, F2O, C2G, F2G,
           PN, PZ, PXS, PXR, PGS, PGR, PA, S0, S1, Q2, Q1, P2, X2C, X2F,
           DIN, ZIN, VIN, ssem, rsem, gssem, grsem, isem):
    loads = [pltpu.make_async_copy(src, dst, isem.at[n])
             for n, (src, dst) in enumerate(((zon_ref, ZIN), (den_ref, DIN), (div_ref, VIN)))]
    for load in loads:
        load.start()
    h = lax.axis_index("height")
    j = lax.axis_index("plan")
    base = h - W if window else 0

    def exists(dh, dj):
        ok = None
        for at, step, count in ((h, dh, H), (j, dj, PL)):
            if step > 0:
                term = at + step < count
            elif step < 0:
                term = at + step >= 0
            else:
                continue
            ok = term if ok is None else jnp.logical_and(ok, term)
        return ok

    barrier = pltpu.get_barrier_semaphore()
    if window:
        for dh in range(-W, W + 1):
            @pl.when(jnp.logical_and(h + dh >= 0, h + dh < H))
            def _():
                for dj in range(PL):
                    if (dh, dj) != (0, 0):
                        pl.semaphore_signal(barrier, inc=1, device_id=(h + dh, wrap(j + dj, PL)), device_id_type=MESH)
    else:
        for a in range(H):
            for b in range(PL):
                if (a, b) != (0, 0):
                    pl.semaphore_signal(barrier, inc=1, device_id=(wrap(h + a, H), wrap(j + b, PL)), device_id_type=MESH)

    ys = lax.broadcasted_iota(jnp.int32, (512, 512), 0)
    cs = lax.broadcasted_iota(jnp.int32, (512, 512), 1)
    order = (ys == 4 * (cs % LANES) + cs // LANES).astype(F32).astype(jnp.bfloat16)
    for load in loads:
        load.wait()
    zones = ZIN[...]
    perm = jnp.zeros(zones.shape, F32)
    for zone_id, value in enumerate(PERMEABILITY):
        perm = jnp.where(zones == zone_id, F32(value), perm)
    cond = perm * inverse(DIN[...])
    both = jnp.concatenate([cond.reshape(64, 512), VIN[...].reshape(64, 512)], axis=0)
    moved = jnp.dot(split3(both), order, preferred_element_type=F32)
    moved = moved[0:128] + moved[128:256] + moved[256:384]
    for v in range(4):
        part = moved[:, v * LANES:(v + 1) * LANES]
        CN[:, v] = part[0:64].reshape(4, 16, LANES)
        DN[:, v] = part[64:128].reshape(4, 16, LANES)
    c = CN[...]
    d = DN[...]
    XS[0, :, :, 0:3] = c[:, :, 13:16]
    XS[0, :, :, 3:5] = d[:, :, 14:16]
    XS[1, :, :, 0:3] = c[:, :, 0:3]
    XS[1, :, :, 3:5] = d[:, :, 0:2]
    for n, (dh, dj) in enumerate(DIAGONALS):
        near, far = (3, 2) if dh > 0 else (0, 1)
        row = 15 if dj > 0 else 0
        two = 14 if dj > 0 else 0
        GS[n, :, 0:2] = c[near, :, two:two + 2]
        GS[n, :, 2:3] = c[far, :, row:row + 1]
        GS[n, :, 3:4] = d[near, :, row:row + 1]

    index = [0]

    def copies(items):
        made = []
        for dh, dj, src, dst in items:
            n = index[0]
            index[0] += 1
            copy = pltpu.make_async_remote_copy(
                src_ref=src, dst_ref=dst, send_sem=ssem.at[n], recv_sem=rsem.at[n],
                device_id=(h + dh, j + dj), device_id_type=MESH)
            made.append((exists(dh, dj), exists(-dh, -dj), copy))
        return made

    def start(made):
        for there, _, copy in made:
            pl.when(there)(copy.start)

    def arrive(made):
        for _, back, copy in made:
            pl.when(back)(copy.wait_recv)

    def sent(made):
        for there, _, copy in made:
            pl.when(there)(copy.wait_send)

    def tiles(ref, around, rows):
        items = []
        for dh, dj in around:
            z0, z1 = {2: (5, 6), -2: (4, 5)}.get(dh, (4, 6))
            x0, x1 = {1: (16 - rows, 16), -1: (8, 8 + rows)}.get(dj, (8, 16))
            items.append((dh, dj, ref.at[z0:z1, :, x0:x1],
                          ref.at[z0 - 2 * dh:z1 - 2 * dh, :, x0 - 8 * dj:x1 - 8 * dj]))
        return copies(items)

    def gather_loop(act):
        if window:
            for dh in range(-W, W + 1):
                for b in range(PL):
                    if (dh, b) != (0, 0):
                        yes = jnp.logical_and(h + dh >= 0, h + dh < H)
                        pl.when(yes)(functools.partial(act, dh, b))
        else:
            for a in range(H):
                for b in range(PL):
                    if (a, b) != (0, 0):
                        act(a, b)

    def gather_copy(which, src, buf, a, b):
        if window:
            to, mine, n = h + a, W - a, a + W
        else:
            to, mine, n = wrap(h + a, H), h, a
        return pltpu.make_async_remote_copy(
            src_ref=src, dst_ref=buf.at[mine, j], send_sem=gssem.at[which, n, b],
            recv_sem=grsem.at[which, n, b], device_id=(to, wrap(j + b, PL)), device_id_type=MESH)

    def gather_in(which, src, buf, a, b):
        gather_copy(which, src, buf, a, b).wait_recv()

    def gather_in_loop(which, src, buf):
        if window:
            for dh in range(-W, W + 1):
                for b in range(PL):
                    if (dh, b) != (0, 0):
                        yes = jnp.logical_and(h - dh >= 0, h - dh < H)
                        pl.when(yes)(functools.partial(gather_in, which, src, buf, dh, b))
        else:
            gather_loop(functools.partial(gather_in, which, src, buf))

    count = None
    if window:
        low = jnp.minimum(h, W)
        high = jnp.minimum(H - 1 - h, W)
        count = (low + high + 1) * PL - 1
    else:
        count = H * PL - 1
    pl.semaphore_wait(barrier, count)

    first = copies(
        [(1, 0, CN.at[1:4], ZC.at[0]), (-1, 0, CN.at[0:3], ZC.at[1]),
         (1, 0, DN.at[2:4], ZD.at[0]), (-1, 0, DN.at[0:2], ZD.at[1]),
         (0, 1, XS.at[0, :, :, 0:5], XR.at[0, :, :, 0:5]), (0, -1, XS.at[1, :, :, 0:5], XR.at[1, :, :, 0:5])]
        + [(dh, dj, GS.at[n, :, 0:4], GR.at[n, :, 0:4]) for n, (dh, dj) in enumerate(DIAGONALS)])
    start(first)

    def pair_rows(ref, first_row, rows):
        return ref[:, :, pl.ds(first_row, rows, stride=2), :] + ref[:, :, pl.ds(first_row + 1, rows, stride=2), :]

    S0[:, :, 4:20] = paired(c)
    own1 = 0.125 * pair_rows(S0, 4, 8)
    C1[4:6, :, 8:16] = own1
    S1[:, :, 8:16] = paired(own1)
    C2O[...] = 0.125 * pair_rows(S1, 8, 4)[0, 0]
    cond1 = tiles(C1, WIDE, 3)
    start(cond1)

    CA[3:7, :, 4:20] = c
    DA[2:6, :, 4:20] = d
    arrive(first)
    CA[0:3, :, 4:20] = ZC[0]
    CA[7:10, :, 4:20] = ZC[1]
    DA[0:2, :, 4:20] = ZD[0]
    DA[6:8, :, 4:20] = ZD[1]
    CA[3:7, :, 1:4] = XR[0, :, :, 0:3]
    CA[3:7, :, 20:23] = XR[1, :, :, 0:3]
    DA[2:6, :, 2:4] = XR[0, :, :, 3:5]
    DA[2:6, :, 20:22] = XR[1, :, :, 3:5]
    for n, (dh, dj) in enumerate(DIAGONALS):
        near, far, dnear = (2, 1, 1) if dh > 0 else (7, 8, 6)
        two, row = (2, 3) if dj > 0 else (20, 20)
        CA[near, :, two:two + 2] = GR[n, :, 0:2]
        CA[far, :, row:row + 1] = GR[n, :, 2:3]
        DA[dnear, :, row:row + 1] = GR[n, :, 3:4]

    def inside(z_count, z_first, z_total, rows, x_first, x_total):
        z = z_first + lax.broadcasted_iota(jnp.int32, (z_count, 1, rows, LANES), 0)
        x = x_first + lax.broadcasted_iota(jnp.int32, (z_count, 1, rows, LANES), 2)
        return (z >= 0) & (z < z_total) & (x >= 0) & (x < x_total)

    in0 = inside(10, 4 * h - 3, 4 * H, 24, 16 * j - 4, 16 * PL)
    k0 = setup(jnp.where(in0, CA[...], 1.0), in0[1:-1])
    f0 = jnp.where(in0[1:-1], DA[...], 0.0)
    p = k0[6] * f0
    k0 = trim(k0)
    f0 = f0[1:-1]
    p = sweep(p, f0, k0)
    PA[1:7] = p
    k0own = trim(k0)
    f0own = f0[1:-1]
    S0[...] = paired(residual(p, f0own, k0own))
    F1[4:6, :, 8:16] = 0.5 * pair_rows(S0, 4, 8)
    second = tiles(F1, AROUND, 2)
    start(second)

    PN[...] = p[1:5, :, 4:20]
    for z in range(4):
        PXS[0, :, z:z + 1] = p[1 + z, :, 18:19]
        PXS[1, :, z:z + 1] = p[1 + z, :, 5:6]
    for n, (dh, dj) in enumerate(DIAGONALS):
        z = 4 if dh > 0 else 1
        row = 19 if dj > 0 else 4
        PGS[n, :, 0:1] = p[z, :, row:row + 1]
    spread = copies(
        [(1, 0, PN.at[2:3], PZ.at[0]), (-1, 0, PN.at[1:2], PZ.at[1]),
         (0, 1, PXS.at[0, :, 0:4], PXR.at[0, :, 0:4]), (0, -1, PXS.at[1, :, 0:4], PXR.at[1, :, 0:4])]
        + [(dh, dj, PGS.at[n, :, 0:1], PGR.at[n, :, 0:1]) for n, (dh, dj) in enumerate(DIAGONALS)])
    start(spread)

    gather_loop(lambda a, b: gather_copy(0, C2O, C2G, a, b).start())

    arrive(cond1)
    in1 = inside(8, 2 * h - 3, 2 * H, 24, 8 * j - 8, 8 * PL)
    k1 = setup(jnp.where(in1, C1[1:9], 1.0), in1[1:-1])
    arrive(second)
    f1 = jnp.where(in1[1:-1], F1[2:8], 0.0)
    p1 = k1[6] * f1
    k1in = trim(k1)
    f1in = f1[1:-1]
    p1 = sweep(p1, f1in, k1in)
    P1[4:6, :, 8:16] = p1[1:3, :, 8:16]
    S1[...] = paired(residual(p1, f1in[1:-1], trim(k1in)))
    F2O[...] = 0.5 * pair_rows(S1, 8, 4)[0, 0]
    gather_loop(lambda a, b: gather_copy(1, F2O, F2G, a, b).start())
    third = tiles(P1, WIDE, 3)
    start(third)

    def own_slot(ref):
        return ref.at[W if window else h, j]

    own_slot(C2G)[...] = C2O[...]
    own_slot(F2G)[...] = F2O[...]
    gather_in_loop(0, C2O, C2G)
    for b in range(PL):
        X2C[:, 4 * b:4 * b + 4, :] = C2G[:, b]
    zz = base + lax.broadcasted_iota(jnp.int32, (layers, 4 * PL, LANES), 0)
    in2 = (zz >= 0) & (zz < H)
    row = lax.broadcasted_iota(jnp.int32, (layers, 4 * PL, LANES), 1)

    def z_prev2(a, fill):
        return jnp.concatenate([jnp.full_like(a[:1], fill), a[:-1]], axis=0)

    def z_next2(a, fill):
        return jnp.concatenate([a[1:], jnp.full_like(a[:1], fill)], axis=0)

    def x_prev2(a, fill):
        return jnp.where(row == 0, fill, x_prev(a))

    def x_next2(a, fill):
        return jnp.where(row == 4 * PL - 1, fill, x_next(a))

    c2 = jnp.where(in2, X2C[...], 1.0)
    edge = harmonic(c2, jnp.ones_like(c2))
    zl = harmonic(c2, z_prev2(c2, 1.0))
    zu = jnp.concatenate([zl[1:], edge[-1:]], axis=0)
    xl = harmonic(c2, x_prev2(c2, 1.0))
    xu = jnp.where(row == 4 * PL - 1, edge, x_next(xl))
    yl = harmonic(c2, lane_prev(c2, 1.0))
    yu = lane_next(yl, edge)
    diag2 = zl + zu + xl + xu + yl + yu
    w2 = jnp.where(in2, OMEGA * inverse(diag2), 0.0)
    share = jnp.sum(diag2, axis=1, keepdims=True)

    def gathered2(q):
        return (zl * z_prev2(q, 0.0) + zu * z_next2(q, 0.0) + xl * x_prev2(q, 0.0) + xu * x_next2(q, 0.0)
                + yl * lane_prev(q, 0.0) + yu * lane_next(q, 0.0))

    gather_in_loop(1, F2O, F2G)
    for b in range(PL):
        X2F[:, 4 * b:4 * b + 4, :] = F2G[:, b]
    f2 = jnp.where(in2, X2F[...], 0.0)
    p2 = w2 * f2
    for _ in range(3):
        p2 = KEEP * p2 + w2 * (f2 + gathered2(p2))
    r2 = f2 - diag2 * p2 + gathered2(p2)
    line = jnp.sum(r2, axis=1, keepdims=True) / share
    p2 = jnp.where(in2, p2 + line, 0.0)
    blank = jnp.zeros((2, 4 * PL, LANES), F32)
    P2[0:2] = blank
    P2[2:2 + layers] = p2
    P2[2 + layers:4 + layers] = blank
    near2 = P2[pl.ds(W if window else h, 5)]
    side = jnp.zeros((5, 4, LANES), F32)
    wide2 = jnp.concatenate([side, near2, side], axis=1)
    mine2 = wide2[:, 0:12]
    for b in range(1, PL):
        mine2 = jnp.where(j == b, wide2[:, 4 * b:4 * b + 12], mine2)
    Q2[:, pl.ds(0, 12, stride=2), :] = mine2
    Q2[:, pl.ds(1, 12, stride=2), :] = mine2
    up2 = Q2[...]
    up2 = jnp.stack([up2[q] for q in (0, 1, 1, 2, 2, 3, 3, 4)], axis=0)[:, None]

    arrive(third)
    p1 = jnp.where(in1, P1[1:9] + up2, 0.0)
    p1 = sweep(p1, f1, k1)
    p1 = sweep(p1, f1in, k1in)
    Q1[:, :, pl.ds(0, 12, stride=2), :] = p1[:, :, 6:18]
    Q1[:, :, pl.ds(1, 12, stride=2), :] = p1[:, :, 6:18]
    up1 = Q1[...]

    arrive(spread)
    PA[0, :, 4:20] = PZ[0, 0]
    PA[7, :, 4:20] = PZ[1, 0]
    for z in range(4):
        PA[2 + z, :, 2:3] = PXR[0, :, z:z + 1]
        PA[2 + z, :, 21:22] = PXR[1, :, z:z + 1]
    for n, (dh, dj) in enumerate(DIAGONALS):
        z = 1 if dh > 0 else 6
        at = 3 if dj > 0 else 20
        PA[z, :, at:at + 1] = PGR[n, :, 0:1]
    fine = jnp.stack([jnp.stack([up1[z // 2, v // 2] for v in range(4)], axis=0) for z in range(8)], axis=0)
    p = jnp.where(in0[1:-1], PA[...] + fine, 0.0)
    p = sweep(p, f0, k0)
    p = sweep(p, f0own, k0own)
    p = p[:, :, 4:20]
    flat = jnp.concatenate([p[:, v].reshape(64, LANES) for v in range(4)], axis=1)
    back = lax.dot_general(split3(flat), order, (((1,), (1,)), ((), ())), preferred_element_type=F32)
    out_ref[...] = (back[0:64] + back[64:128] + back[128:192]).reshape(4, 16, 512)

    for made in (first, cond1, second, spread, third):
        sent(made)
    gather_loop(lambda a, b: gather_copy(0, C2O, C2G, a, b).wait_send())
    gather_loop(lambda a, b: gather_copy(1, F2O, F2G, a, b).wait_send())


def solution(mesh):
    H = mesh.shape["height"]
    PL = mesh.shape["plan"]
    window = H > 15
    W = 7
    layers = 2 * W + 1 if window else H
    copies = 10 + len(WIDE) + len(AROUND) + 8 + len(WIDE)

    def v(*shape):
        return pltpu.VMEM(shape + (LANES,), F32)

    scratch = [
        v(4, 4, 16), v(4, 4, 16),
        v(2, 3, 4, 16), v(2, 2, 4, 16),
        v(2, 4, 4, 8), v(2, 4, 4, 8),
        v(4, 4, 8), v(4, 4, 8),
        v(10, 4, 24), v(8, 4, 24),
        v(10, 2, 24), v(10, 2, 24), v(10, 2, 24),
        v(4), v(4), v(layers, PL, 4), v(layers, PL, 4),
        v(4, 4, 16), v(2, 1, 4, 16),
        v(2, 4, 8), v(2, 4, 8),
        v(4, 4, 8), v(4, 4, 8),
        v(8, 4, 24),
        v(2, 2, 24), v(1, 1, 24),
        v(5, 24), v(4, 2, 24),
        v(layers + 4, 4 * PL), v(layers, 4 * PL), v(layers, 4 * PL),
        pltpu.VMEM((4, 16, 512), F32), pltpu.VMEM((4, 16, 512), jnp.int32), pltpu.VMEM((4, 16, 512), F32),
        pltpu.SemaphoreType.DMA((copies,)), pltpu.SemaphoreType.DMA((copies,)),
        pltpu.SemaphoreType.DMA((2, layers, PL)), pltpu.SemaphoreType.DMA((2, layers, PL)),
        pltpu.SemaphoreType.DMA((3,)),
    ]

    def on_device(divergence, density, zones):
        return pl.pallas_call(
            functools.partial(kernel, H, PL, W, layers, window),
            out_shape=jax.ShapeDtypeStruct(divergence.shape, F32),
            in_specs=[pl.BlockSpec(memory_space=pltpu.HBM)] * 3,
            out_specs=pl.BlockSpec(memory_space=pltpu.VMEM),
            scratch_shapes=scratch,
            compiler_params=pltpu.CompilerParams(
                collective_id=0, has_side_effects=True),
            cost_estimate=pl.CostEstimate(flops=20_000_000, bytes_accessed=1_000_000, transcendentals=0),
            name="v_cycle",
        )(divergence, density, zones)

    spec = P("height", "plan", None)
    return jax.shard_map(on_device, mesh=mesh, in_specs=(spec, spec, spec), out_specs=spec, check_vma=False)
```

```python
import functools

import jax
import jax.numpy as jnp
from jax import lax
from jax.experimental import pallas as pl
from jax.experimental.pallas import tpu as pltpu
from jax.sharding import PartitionSpec as P

PERMEABILITY = (1.0, 0.1, 0.6, 0.8, 0.25)
OMEGA = 2.0 / 3.0
KEEP = 1.0 / 3.0
MESH = pl.DeviceIdType.MESH
F32 = jnp.float32
LANES = 128

SIDES = (1, -1)
DIAGONALS = ((1, 1), (1, -1), (-1, 1), (-1, -1))
AROUND = tuple((a, b) for a in (-1, 0, 1) for b in (-1, 0, 1) if (a, b) != (0, 0))
WIDE = tuple((a, b) for a in (-2, -1, 0, 1, 2) for b in (-1, 0, 1) if (a, b) != (0, 0))


def inverse(a):
    r = pl.reciprocal(a, approx=True)
    return r * (2.0 - a * r)


def harmonic(a, b):
    return (2.0 * a * b) * inverse(a + b)


def wrap(a, count):
    return jnp.where(a >= count, a - count, a)


def lane_of(a):
    return lax.broadcasted_iota(jnp.int32, a.shape, a.ndim - 1)


def lane_prev(a, fill):
    return jnp.where(lane_of(a) == 0, fill, pltpu.roll(a, 1, a.ndim - 1))


def lane_next(a, fill):
    return jnp.where(lane_of(a) == LANES - 1, fill, pltpu.roll(a, LANES - 1, a.ndim - 1))


def y_prev(a, fill):
    return jnp.concatenate([lane_prev(a[:, -1:], fill), a[:, :-1]], axis=1)


def y_next(a, fill):
    return jnp.concatenate([a[:, 1:], lane_next(a[:, :1], fill)], axis=1)


def x_prev(a):
    return pltpu.roll(a, 1, a.ndim - 2)


def x_next(a):
    return pltpu.roll(a, a.shape[-2] - 1, a.ndim - 2)


def setup(c, inside):
    cz = harmonic(c[:-1], c[1:])
    m = c[1:-1]
    cx = harmonic(m, x_next(m))
    cxl = x_prev(cx)
    cyl = harmonic(m, y_prev(m, 1.0))
    cyu = y_next(cyl, harmonic(m[:, -1:], jnp.ones_like(m[:, -1:])))
    diag = cz[:-1] + cz[1:] + cx + cxl + cyl + cyu
    w = jnp.where(inside, OMEGA * inverse(diag), 0.0)
    return (cz, cx, cxl, cyl, cyu, diag, w)


def trim(k):
    return tuple(part[1:-1] for part in k)


def gathered(p, k):
    cz, cx, cxl, cyl, cyu = k[:5]
    m = p[1:-1]
    return (cz[:-1] * p[:-2] + cz[1:] * p[2:] + cx * x_next(m) + cxl * x_prev(m)
            + cyl * y_prev(m, 0.0) + cyu * y_next(m, 0.0))


def sweep(p, f, k):
    return KEEP * p[1:-1] + k[6] * (f + gathered(p, k))


def residual(p, f, k):
    return f - k[5] * p[1:-1] + gathered(p, k)


def paired(a):
    z, v = a.shape[:2]
    rows = []
    for i in range(0, z, 2):
        both = a[i] + a[i + 1]
        rows.append(jnp.stack([both[q] + both[q + 1] for q in range(0, v, 2)], axis=0))
    return jnp.stack(rows, axis=0)


def split3(a):
    one = a.astype(jnp.bfloat16)
    rest = a - one.astype(F32)
    two = rest.astype(jnp.bfloat16)
    three = (rest - two.astype(F32)).astype(jnp.bfloat16)
    return jnp.concatenate([one, two, three], axis=0)


def kernel(H, PL, W, layers, window, div_ref, den_ref, zon_ref, out_ref,
           CN, DN, ZC, ZD, XS, XR, GS, GR, CA, DA, C1, F1, P1, C2O, F2O, C2G, F2G,
           PN, PZ, PXS, PXR, PGS, PGR, PA, S0, S1, Q2, Q1, P2, X2C, X2F,
           DIN, ZIN, VIN, ssem, rsem, gssem, grsem, isem):
    loads = [pltpu.make_async_copy(src, dst, isem.at[n])
             for n, (src, dst) in enumerate(((zon_ref, ZIN), (den_ref, DIN), (div_ref, VIN)))]
    for load in loads:
        load.start()
    h = lax.axis_index("height")
    j = lax.axis_index("plan")
    base = h - W if window else 0

    def exists(dh, dj):
        ok = None
        for at, step, count in ((h, dh, H), (j, dj, PL)):
            if step > 0:
                term = at + step < count
            elif step < 0:
                term = at + step >= 0
            else:
                continue
            ok = term if ok is None else jnp.logical_and(ok, term)
        return ok

    barrier = pltpu.get_barrier_semaphore()
    if window:
        for dh in range(-W, W + 1):
            @pl.when(jnp.logical_and(h + dh >= 0, h + dh < H))
            def _():
                for dj in range(PL):
                    if (dh, dj) != (0, 0):
                        pl.semaphore_signal(barrier, inc=1, device_id=(h + dh, wrap(j + dj, PL)), device_id_type=MESH)
    else:
        for a in range(H):
            for b in range(PL):
                if (a, b) != (0, 0):
                    pl.semaphore_signal(barrier, inc=1, device_id=(wrap(h + a, H), wrap(j + b, PL)), device_id_type=MESH)

    ys = lax.broadcasted_iota(jnp.int32, (512, 512), 0)
    cs = lax.broadcasted_iota(jnp.int32, (512, 512), 1)
    order = (ys == 4 * (cs % LANES) + cs // LANES).astype(F32).astype(jnp.bfloat16)
    for load in loads:
        load.wait()
    zones = ZIN[...]
    perm = jnp.zeros(zones.shape, F32)
    for zone_id, value in enumerate(PERMEABILITY):
        perm = jnp.where(zones == zone_id, F32(value), perm)
    cond = perm * inverse(DIN[...])
    both = jnp.concatenate([cond.reshape(64, 512), VIN[...].reshape(64, 512)], axis=0)
    moved = jnp.dot(split3(both), order, preferred_element_type=F32)
    moved = moved[0:128] + moved[128:256] + moved[256:384]
    for v in range(4):
        part = moved[:, v * LANES:(v + 1) * LANES]
        CN[:, v] = part[0:64].reshape(4, 16, LANES)
        DN[:, v] = part[64:128].reshape(4, 16, LANES)
    c = CN[...]
    d = DN[...]
    XS[0, :, :, 0:3] = c[:, :, 13:16]
    XS[0, :, :, 3:5] = d[:, :, 14:16]
    XS[1, :, :, 0:3] = c[:, :, 0:3]
    XS[1, :, :, 3:5] = d[:, :, 0:2]
    for n, (dh, dj) in enumerate(DIAGONALS):
        near, far = (3, 2) if dh > 0 else (0, 1)
        row = 15 if dj > 0 else 0
        two = 14 if dj > 0 else 0
        GS[n, :, 0:2] = c[near, :, two:two + 2]
        GS[n, :, 2:3] = c[far, :, row:row + 1]
        GS[n, :, 3:4] = d[near, :, row:row + 1]

    index = [0]

    def copies(items):
        made = []
        for dh, dj, src, dst in items:
            n = index[0]
            index[0] += 1
            copy = pltpu.make_async_remote_copy(
                src_ref=src, dst_ref=dst, send_sem=ssem.at[n], recv_sem=rsem.at[n],
                device_id=(h + dh, j + dj), device_id_type=MESH)
            made.append((exists(dh, dj), exists(-dh, -dj), copy))
        return made

    def start(made):
        for there, _, copy in made:
            pl.when(there)(copy.start)

    def arrive(made):
        for _, back, copy in made:
            pl.when(back)(copy.wait_recv)

    def sent(made):
        for there, _, copy in made:
            pl.when(there)(copy.wait_send)

    def tiles(ref, around, rows):
        items = []
        for dh, dj in around:
            z0, z1 = {2: (5, 6), -2: (4, 5)}.get(dh, (4, 6))
            x0, x1 = {1: (16 - rows, 16), -1: (8, 8 + rows)}.get(dj, (8, 16))
            items.append((dh, dj, ref.at[z0:z1, :, x0:x1],
                          ref.at[z0 - 2 * dh:z1 - 2 * dh, :, x0 - 8 * dj:x1 - 8 * dj]))
        return copies(items)

    def gather_loop(act):
        if window:
            for dh in range(-W, W + 1):
                for b in range(PL):
                    if (dh, b) != (0, 0):
                        yes = jnp.logical_and(h + dh >= 0, h + dh < H)
                        pl.when(yes)(functools.partial(act, dh, b))
        else:
            for a in range(H):
                for b in range(PL):
                    if (a, b) != (0, 0):
                        act(a, b)

    def gather_copy(which, src, buf, a, b):
        if window:
            to, mine, n = h + a, W - a, a + W
        else:
            to, mine, n = wrap(h + a, H), h, a
        return pltpu.make_async_remote_copy(
            src_ref=src, dst_ref=buf.at[mine, j], send_sem=gssem.at[which, n, b],
            recv_sem=grsem.at[which, n, b], device_id=(to, wrap(j + b, PL)), device_id_type=MESH)

    def gather_in(which, src, buf, a, b):
        gather_copy(which, src, buf, a, b).wait_recv()

    def gather_in_loop(which, src, buf):
        if window:
            for dh in range(-W, W + 1):
                for b in range(PL):
                    if (dh, b) != (0, 0):
                        yes = jnp.logical_and(h - dh >= 0, h - dh < H)
                        pl.when(yes)(functools.partial(gather_in, which, src, buf, dh, b))
        else:
            gather_loop(functools.partial(gather_in, which, src, buf))

    count = None
    if window:
        low = jnp.minimum(h, W)
        high = jnp.minimum(H - 1 - h, W)
        count = (low + high + 1) * PL - 1
    else:
        count = H * PL - 1
    pl.semaphore_wait(barrier, count)

    first = copies(
        [(1, 0, CN.at[1:4], ZC.at[0]), (-1, 0, CN.at[0:3], ZC.at[1]),
         (1, 0, DN.at[2:4], ZD.at[0]), (-1, 0, DN.at[0:2], ZD.at[1]),
         (0, 1, XS.at[0, :, :, 0:5], XR.at[0, :, :, 0:5]), (0, -1, XS.at[1, :, :, 0:5], XR.at[1, :, :, 0:5])]
        + [(dh, dj, GS.at[n, :, 0:4], GR.at[n, :, 0:4]) for n, (dh, dj) in enumerate(DIAGONALS)])
    start(first)

    def pair_rows(ref, first_row, rows):
        return ref[:, :, pl.ds(first_row, rows, stride=2), :] + ref[:, :, pl.ds(first_row + 1, rows, stride=2), :]

    S0[:, :, 4:20] = paired(c)
    own1 = 0.125 * pair_rows(S0, 4, 8)
    C1[4:6, :, 8:16] = own1
    S1[:, :, 8:16] = paired(own1)
    C2O[...] = 0.125 * pair_rows(S1, 8, 4)[0, 0]
    cond1 = tiles(C1, WIDE, 3)
    start(cond1)

    CA[3:7, :, 4:20] = c
    DA[2:6, :, 4:20] = d
    arrive(first)
    CA[0:3, :, 4:20] = ZC[0]
    CA[7:10, :, 4:20] = ZC[1]
    DA[0:2, :, 4:20] = ZD[0]
    DA[6:8, :, 4:20] = ZD[1]
    CA[3:7, :, 1:4] = XR[0, :, :, 0:3]
    CA[3:7, :, 20:23] = XR[1, :, :, 0:3]
    DA[2:6, :, 2:4] = XR[0, :, :, 3:5]
    DA[2:6, :, 20:22] = XR[1, :, :, 3:5]
    for n, (dh, dj) in enumerate(DIAGONALS):
        near, far, dnear = (2, 1, 1) if dh > 0 else (7, 8, 6)
        two, row = (2, 3) if dj > 0 else (20, 20)
        CA[near, :, two:two + 2] = GR[n, :, 0:2]
        CA[far, :, row:row + 1] = GR[n, :, 2:3]
        DA[dnear, :, row:row + 1] = GR[n, :, 3:4]

    def inside(z_count, z_first, z_total, rows, x_first, x_total):
        z = z_first + lax.broadcasted_iota(jnp.int32, (z_count, 1, rows, LANES), 0)
        x = x_first + lax.broadcasted_iota(jnp.int32, (z_count, 1, rows, LANES), 2)
        return (z >= 0) & (z < z_total) & (x >= 0) & (x < x_total)

    in0 = inside(10, 4 * h - 3, 4 * H, 24, 16 * j - 4, 16 * PL)
    k0 = setup(jnp.where(in0, CA[...], 1.0), in0[1:-1])
    f0 = jnp.where(in0[1:-1], DA[...], 0.0)
    p = k0[6] * f0
    k0 = trim(k0)
    f0 = f0[1:-1]
    p = sweep(p, f0, k0)
    PA[1:7] = p
    k0own = trim(k0)
    f0own = f0[1:-1]
    S0[...] = paired(residual(p, f0own, k0own))
    F1[4:6, :, 8:16] = 0.5 * pair_rows(S0, 4, 8)
    second = tiles(F1, AROUND, 2)
    start(second)

    PN[...] = p[1:5, :, 4:20]
    for z in range(4):
        PXS[0, :, z:z + 1] = p[1 + z, :, 18:19]
        PXS[1, :, z:z + 1] = p[1 + z, :, 5:6]
    for n, (dh, dj) in enumerate(DIAGONALS):
        z = 4 if dh > 0 else 1
        row = 19 if dj > 0 else 4
        PGS[n, :, 0:1] = p[z, :, row:row + 1]
    spread = copies(
        [(1, 0, PN.at[2:3], PZ.at[0]), (-1, 0, PN.at[1:2], PZ.at[1]),
         (0, 1, PXS.at[0, :, 0:4], PXR.at[0, :, 0:4]), (0, -1, PXS.at[1, :, 0:4], PXR.at[1, :, 0:4])]
        + [(dh, dj, PGS.at[n, :, 0:1], PGR.at[n, :, 0:1]) for n, (dh, dj) in enumerate(DIAGONALS)])
    start(spread)

    gather_loop(lambda a, b: gather_copy(0, C2O, C2G, a, b).start())

    arrive(cond1)
    in1 = inside(8, 2 * h - 3, 2 * H, 24, 8 * j - 8, 8 * PL)
    k1 = setup(jnp.where(in1, C1[1:9], 1.0), in1[1:-1])
    arrive(second)
    f1 = jnp.where(in1[1:-1], F1[2:8], 0.0)
    p1 = k1[6] * f1
    k1in = trim(k1)
    f1in = f1[1:-1]
    p1 = sweep(p1, f1in, k1in)
    P1[4:6, :, 8:16] = p1[1:3, :, 8:16]
    S1[...] = paired(residual(p1, f1in[1:-1], trim(k1in)))
    F2O[...] = 0.5 * pair_rows(S1, 8, 4)[0, 0]
    gather_loop(lambda a, b: gather_copy(1, F2O, F2G, a, b).start())
    third = tiles(P1, WIDE, 3)
    start(third)

    def own_slot(ref):
        return ref.at[W if window else h, j]

    own_slot(C2G)[...] = C2O[...]
    own_slot(F2G)[...] = F2O[...]
    gather_in_loop(0, C2O, C2G)
    for b in range(PL):
        X2C[:, 4 * b:4 * b + 4, :] = C2G[:, b]
    zz = base + lax.broadcasted_iota(jnp.int32, (layers, 4 * PL, LANES), 0)
    in2 = (zz >= 0) & (zz < H)
    row = lax.broadcasted_iota(jnp.int32, (layers, 4 * PL, LANES), 1)

    def z_prev2(a, fill):
        return jnp.concatenate([jnp.full_like(a[:1], fill), a[:-1]], axis=0)

    def z_next2(a, fill):
        return jnp.concatenate([a[1:], jnp.full_like(a[:1], fill)], axis=0)

    def x_prev2(a, fill):
        return jnp.where(row == 0, fill, x_prev(a))

    def x_next2(a, fill):
        return jnp.where(row == 4 * PL - 1, fill, x_next(a))

    c2 = jnp.where(in2, X2C[...], 1.0)
    edge = harmonic(c2, jnp.ones_like(c2))
    zl = harmonic(c2, z_prev2(c2, 1.0))
    zu = jnp.concatenate([zl[1:], edge[-1:]], axis=0)
    xl = harmonic(c2, x_prev2(c2, 1.0))
    xu = jnp.where(row == 4 * PL - 1, edge, x_next(xl))
    yl = harmonic(c2, lane_prev(c2, 1.0))
    yu = lane_next(yl, edge)
    diag2 = zl + zu + xl + xu + yl + yu
    w2 = jnp.where(in2, OMEGA * inverse(diag2), 0.0)
    share = jnp.sum(diag2, axis=1, keepdims=True)

    def gathered2(q):
        return (zl * z_prev2(q, 0.0) + zu * z_next2(q, 0.0) + xl * x_prev2(q, 0.0) + xu * x_next2(q, 0.0)
                + yl * lane_prev(q, 0.0) + yu * lane_next(q, 0.0))

    for made in (first, cond1, second, spread):
        sent(made)
    gather_loop(lambda a, b: gather_copy(0, C2O, C2G, a, b).wait_send())
    gather_in_loop(1, F2O, F2G)
    for b in range(PL):
        X2F[:, 4 * b:4 * b + 4, :] = F2G[:, b]
    f2 = jnp.where(in2, X2F[...], 0.0)
    p2 = w2 * f2
    for _ in range(3):
        p2 = KEEP * p2 + w2 * (f2 + gathered2(p2))
    r2 = f2 - diag2 * p2 + gathered2(p2)
    line = jnp.sum(r2, axis=1, keepdims=True) / share
    p2 = jnp.where(in2, p2 + line, 0.0)
    blank = jnp.zeros((2, 4 * PL, LANES), F32)
    P2[0:2] = blank
    P2[2:2 + layers] = p2
    P2[2 + layers:4 + layers] = blank
    near2 = P2[pl.ds(W if window else h, 5)]
    side = jnp.zeros((5, 4, LANES), F32)
    wide2 = jnp.concatenate([side, near2, side], axis=1)
    mine2 = wide2[:, 0:12]
    for b in range(1, PL):
        mine2 = jnp.where(j == b, wide2[:, 4 * b:4 * b + 12], mine2)
    Q2[:, pl.ds(0, 12, stride=2), :] = mine2
    Q2[:, pl.ds(1, 12, stride=2), :] = mine2
    up2 = Q2[...]
    up2 = jnp.stack([up2[q] for q in (0, 1, 1, 2, 2, 3, 3, 4)], axis=0)[:, None]

    arrive(third)
    p1 = jnp.where(in1, P1[1:9] + up2, 0.0)
    p1 = sweep(p1, f1, k1)
    p1 = sweep(p1, f1in, k1in)
    Q1[:, :, pl.ds(0, 12, stride=2), :] = p1[:, :, 6:18]
    Q1[:, :, pl.ds(1, 12, stride=2), :] = p1[:, :, 6:18]
    up1 = Q1[...]

    arrive(spread)
    PA[0, :, 4:20] = PZ[0, 0]
    PA[7, :, 4:20] = PZ[1, 0]
    for z in range(4):
        PA[2 + z, :, 2:3] = PXR[0, :, z:z + 1]
        PA[2 + z, :, 21:22] = PXR[1, :, z:z + 1]
    for n, (dh, dj) in enumerate(DIAGONALS):
        z = 1 if dh > 0 else 6
        at = 3 if dj > 0 else 20
        PA[z, :, at:at + 1] = PGR[n, :, 0:1]
    fine = jnp.stack([jnp.stack([up1[z // 2, v // 2] for v in range(4)], axis=0) for z in range(8)], axis=0)
    p = jnp.where(in0[1:-1], PA[...] + fine, 0.0)
    p = sweep(p, f0, k0)
    p = sweep(p, f0own, k0own)
    p = p[:, :, 4:20]
    flat = jnp.concatenate([p[:, v].reshape(64, LANES) for v in range(4)], axis=1)
    back = lax.dot_general(split3(flat), order, (((1,), (1,)), ((), ())), preferred_element_type=F32)
    out_ref[...] = (back[0:64] + back[64:128] + back[128:192]).reshape(4, 16, 512)

    sent(third)
    gather_loop(lambda a, b: gather_copy(1, F2O, F2G, a, b).wait_send())


def solution(mesh):
    H = mesh.shape["height"]
    PL = mesh.shape["plan"]
    window = H > 15
    W = 7
    layers = 2 * W + 1 if window else H
    copies = 10 + len(WIDE) + len(AROUND) + 8 + len(WIDE)

    def v(*shape):
        return pltpu.VMEM(shape + (LANES,), F32)

    scratch = [
        v(4, 4, 16), v(4, 4, 16),
        v(2, 3, 4, 16), v(2, 2, 4, 16),
        v(2, 4, 4, 8), v(2, 4, 4, 8),
        v(4, 4, 8), v(4, 4, 8),
        v(10, 4, 24), v(8, 4, 24),
        v(10, 2, 24), v(10, 2, 24), v(10, 2, 24),
        v(4), v(4), v(layers, PL, 4), v(layers, PL, 4),
        v(4, 4, 16), v(2, 1, 4, 16),
        v(2, 4, 8), v(2, 4, 8),
        v(4, 4, 8), v(4, 4, 8),
        v(8, 4, 24),
        v(2, 2, 24), v(1, 1, 24),
        v(5, 24), v(4, 2, 24),
        v(layers + 4, 4 * PL), v(layers, 4 * PL), v(layers, 4 * PL),
        pltpu.VMEM((4, 16, 512), F32), pltpu.VMEM((4, 16, 512), jnp.int32), pltpu.VMEM((4, 16, 512), F32),
        pltpu.SemaphoreType.DMA((copies,)), pltpu.SemaphoreType.DMA((copies,)),
        pltpu.SemaphoreType.DMA((2, layers, PL)), pltpu.SemaphoreType.DMA((2, layers, PL)),
        pltpu.SemaphoreType.DMA((3,)),
    ]

    def on_device(divergence, density, zones):
        return pl.pallas_call(
            functools.partial(kernel, H, PL, W, layers, window),
            out_shape=jax.ShapeDtypeStruct(divergence.shape, F32),
            in_specs=[pl.BlockSpec(memory_space=pltpu.HBM)] * 3,
            out_specs=pl.BlockSpec(memory_space=pltpu.VMEM),
            scratch_shapes=scratch,
            compiler_params=pltpu.CompilerParams(
                collective_id=0, has_side_effects=True),
            cost_estimate=pl.CostEstimate(flops=20_000_000, bytes_accessed=1_000_000, transcendentals=0),
            name="v_cycle",
        )(divergence, density, zones)

    spec = P("height", "plan", None)
    return jax.shard_map(on_device, mesh=mesh, in_specs=(spec, spec, spec), out_specs=spec, check_vma=False)
```
